128 devices in a mesh: pipe: 4 (over z), ed: 32 (over y, x, core).
Axes of the slice: x: 4, y: 4, z: 4, core: 2. Of those that a mesh axis runs over, the one named last changes fastest.
Arguments:
- inputs: bfloat16 [8, 512, 6144], P(None, 'ed', 'pipe'), may hold values from -6 to 6
- gain: bfloat16 [4, 6144], P('pipe'), may hold values from 0.5 to 1.5
- w_up: bfloat16 [4, 6144, 32768], P('pipe', None, 'ed'), may hold values from -0.078125 to 0.078125
- w_down: bfloat16 [4, 32768, 6144], P('pipe', 'ed'), may hold values from -0.0625 to 0.0625
- routes: int32 [4, 8, 512, 2], P('pipe', None, 'ed'), may hold values from 0 to 7, all different within a row; in each aligned block of 16 rows (0 to 15, 16 to 31, ..., all dimensions but the last counted through in order) at most 6 rows name the same one
- route_weight: float32 [4, 8, 512, 2], P('pipe', None, 'ed'), may hold values from 0.1 to 0.9
Outputs:
- hidden_states: bfloat16 [4, 8, 512, 6144], P('pipe', None, 'ed')
The draws below stay inside these ranges and needn't reach their ends.
Inputs may be any that keep to these rules, and one draw needn't show every extreme that they name: `routes`: the two experts of a token differ. In each micro-batch of each section, the 16 tokens of one device name no expert more than 6 times; in some micro-batches an expert is named exactly 6 times there.
All inputs are finite; a program needn't handle non-finite values.
Results may differ from the reference program's by a relative error of at most 0.0095.
Values may be sent and summed in bfloat16 or wider, within the bound.
No kernel may reach another device: no remote copies, remote signals or barrier semaphores. Data moves between devices by JAX's collectives and lax.ppermute only.
A program may use at most 128 MiB of HBM per device.

```python
import math
import jax
import jax.numpy as jnp
import numpy as np
from jax import lax

D = 6144
FF = 8192
ROUTED = 8
EXPERTS = 4
TOK_DEV = 16
MICRO = 8
MOST = 6
SECTIONS = 4
TOKENS = 512
N_ED = 32


def steps_of(stream_key, dims, shards, low, top_value):
    factor_of, own = 1.0, jax.random.fold_in(stream_key, 6)
    for position, shards_of in shards:
        steps = jnp.exp(jax.random.uniform(jax.random.fold_in(own, position), (shards_of,), jnp.float32, low / len(shards), top_value / len(shards)))
        factor_of = factor_of * jnp.repeat(steps, dims[position] // shards_of).reshape([-1 if axis == position else 1 for axis in range(len(dims))])
    return factor_of


def routed_block(own_key, own, number, rows, count, top, reach, skew):
    sequence = jax.random.permutation(own_key, count)
    packed, ordinary = shares(count, rows * top, reach, skew, True), shares(count, rows * top, reach, skew, False)
    places = jnp.arange(count)

    def named(sizes, turn):
        used = int((sizes > 0).sum())
        fixed = max(1, used // 4)
        moved = fixed + (places - fixed + turn * (used - fixed)) % max(1, count - fixed)
        return jnp.zeros((count,), jnp.int32).at[sequence[jnp.where(places < fixed, places, moved)]].set(jnp.asarray(sizes, jnp.int32))

    sizes = jnp.where(number % 4 == 0, named(packed, number // 4), named(ordinary, number - number // 4 - 1))
    mixed = jax.random.permutation(jax.random.fold_in(own, 3), count)
    source_of, sink = mixed[0:count // 2 * 2:2], mixed[1:count // 2 * 2:2]
    margin = jnp.minimum(sizes[source_of] - 1, reach - sizes[sink]) // 2
    margin = jnp.where((source_of == sequence[0]) | (sink == sequence[0]) | (sizes[sink] == 0), 0, jnp.maximum(margin, 0))
    moved = jax.random.randint(jax.random.fold_in(own, 4), (count // 2,), 0, 1 << 20) % (margin + 1)
    sizes = sizes.at[source_of].add(-moved).at[sink].add(moved)
    members = jnp.searchsorted(jnp.cumsum(sizes), jnp.arange(rows * top), side="right").astype(jnp.int32)
    grid = members.reshape(top, rows).T
    grid = grid[jax.random.permutation(jax.random.fold_in(own, 1), rows)]
    turn = jax.random.randint(jax.random.fold_in(own, 2), (rows, 1), 0, top)
    return jnp.take_along_axis(grid, (jnp.arange(top)[None, :] + turn) % top, axis=1)


def shares(count, total, limit, lean, full):
    weights = [(1 << 20) // math.isqrt(rank ** lean) + 1 for rank in range(1, count + 1)]
    largest = limit if full else min(limit, max(-(-total // count), total * weights[0] // sum(weights)))
    least = 1 if total - largest >= count - 1 else 0
    holding, rest = [largest] + [least] * (count - 1), total - largest - least * (count - 1)
    while rest > 0:
        candidates = [i for i in range(1, count) if holding[i] < largest] or [i for i in range(1, count) if holding[i] < limit]
        whole, remaining = sum([weights[i] for i in candidates]), rest
        for i in candidates:
            addition = min(limit - holding[i], max(1, remaining * weights[i] // whole), rest)
            holding[i] = holding[i] + addition
            rest = rest - addition
    return np.array(holding)


def normal_values(key, shape, scale, most, split=(), held_as=jnp.bfloat16):
    array = scale * jax.random.normal(key, shape, jnp.float32)
    if split:
        array = array * steps_of(key, shape, split, -0.22, 0.18)
    return jnp.clip(array, -most, most).astype(held_as)


def setup_inputs(seed: int = 0) -> dict:
    splits = jax.random.split(jax.random.key(seed), 7)
    inputs = normal_values(splits[0], (MICRO, TOKENS, D), 1.0, 6.0, ((1, 32), (2, 4)))
    gain = jnp.clip(0.5 + 1.0 * jax.random.uniform(splits[1], (SECTIONS, D), jnp.float32) ** steps_of(splits[1], (SECTIONS, D), ((0, 4),), -0.2, 0.2), 0.5, 1.5).astype(jnp.bfloat16)
    w_up = normal_values(splits[2], (SECTIONS, D, EXPERTS * FF), D ** -0.5, 0.078125, ((0, 4), (2, 32)))
    w_down = normal_values(splits[3], (SECTIONS, EXPERTS * FF, D), FF ** -0.5, 0.0625, ((0, 4), (1, 32)))
    routes_keys = jax.random.split(jax.random.fold_in(splits[4], 1), SECTIONS * MICRO * TOKENS // TOK_DEV)
    routes_turns = jax.random.permutation(jax.random.fold_in(splits[4], 3), SECTIONS * MICRO * TOKENS // TOK_DEV)
    routes = jax.vmap(lambda own, number: routed_block(jax.random.fold_in(splits[4], 2), own, number, TOK_DEV, ROUTED, 2, MOST, 2))(routes_keys, routes_turns).reshape((SECTIONS, MICRO, TOKENS, 2))
    route_weight = jnp.clip(0.1 + 0.79999997 * jax.random.uniform(splits[5], (SECTIONS, MICRO, TOKENS, 2), jnp.float32) ** steps_of(splits[5], (SECTIONS, MICRO, TOKENS, 2), ((0, 4), (2, 32)), -0.2, 0.2), 0.1, 0.9)
    return {"inputs": inputs, "gain": gain, "w_up": w_up, "w_down": w_down, "routes": routes, "route_weight": route_weight}


def expert_mix(normed, up_s, down_s, chosen, weights):
    group = N_ED // EXPERTS
    slice_width = FF // group
    capacity = N_ED * MOST
    mixed = jnp.zeros((TOKENS, D), jnp.float32)
    for expert in range(EXPERTS):
        named = chosen == expert
        weight_tok = lax.optimization_barrier(jnp.sum(jnp.where(named, weights, jnp.zeros_like(weights)), axis=1))
        hit = jnp.any(named, axis=1)
        index = jnp.nonzero(hit, size=capacity, fill_value=0)[0].astype(jnp.int32)
        valid = jnp.arange(capacity, dtype=jnp.int32) < jnp.sum(hit.astype(jnp.int32))
        rows = jnp.take(normed, index, axis=0)
        up_e = up_s[:, expert * FF:(expert + 1) * FF]
        down_e = down_s[expert * FF:(expert + 1) * FF, :]
        hidden = jax.nn.silu(jnp.dot(rows, up_e, preferred_element_type=jnp.float32)).astype(jnp.bfloat16)
        parts = jnp.einsum('tgf,gfd->tgd', hidden.reshape(-1, group, slice_width).astype(jnp.float32), down_e.reshape(group, slice_width, -1).astype(jnp.float32))
        parts = lax.optimization_barrier(parts.astype(jnp.bfloat16)).astype(jnp.float32)
        expert_out = lax.optimization_barrier(jnp.sum(parts, axis=1))
        term = jnp.take(weight_tok, index, axis=0)[:, None] * expert_out
        term = jnp.where(valid[:, None], term, jnp.zeros_like(term))
        mixed = mixed.at[index].add(term)
    return mixed

def reference(inputs, gain, w_up, w_down, routes, route_weight):
    sections = []
    for section in range(SECTIONS):
        outputs = []
        for micro in range(MICRO):
            panel = inputs[micro] if section == 0 else sections[section - 1][micro]
            values = panel.astype(jnp.float32)
            scale = lax.rsqrt(lax.optimization_barrier(jnp.mean(values * values, axis=-1, keepdims=True)) + 1e-05)
            normed = (values * scale * gain[section].astype(jnp.float32)).astype(jnp.bfloat16)
            mixed = expert_mix(normed, w_up[section], w_down[section], routes[section, micro], route_weight[section, micro])
            outputs.append((values + mixed).astype(jnp.bfloat16))
        sections.append(jnp.stack(outputs))
    return jnp.stack(sections)
```

```python
import functools

import jax
import jax.numpy as jnp
from jax import lax
from jax.experimental import pallas as pl
from jax.experimental.pallas import tpu as pltpu
from jax.sharding import Mesh, PartitionSpec as P

EXPERTS = 4
MOST = 6
PAD = 8
STREAMS = 2
GATHER = False
LIMIT = 10
PERIOD = 75.0
OFFSET = 18.0
PHASES = (0.0, 10.0, 31.0, 40.0, 56.5, 66.0)
SECTIONS = 4
BF = jnp.bfloat16
F32 = jnp.float32


def dot(a, b):
    return jnp.dot(a, b, preferred_element_type=F32)


def whole(n):
    return [pl.BlockSpec(memory_space=pltpu.VMEM)] * n


def moved(value, axis, by):
    n = lax.axis_size(axis)
    return lax.ppermute(value, axis, [(i, (i + by) % n) for i in range(n)])


def stacked(refs):
    return jnp.concatenate([r[...].astype(F32) for r in refs], axis=0).astype(BF)


def joined(parts):
    return jnp.concatenate([p[0].astype(F32) for p in parts], axis=1)


def enter_kernel(step, source, idx, gain, table, *refs):
    ins, outs = refs[: len(refs) - 1 - EXPERTS], refs[len(refs) - 1 - EXPERTS :]
    if source == "inputs":
        values = joined(ins)
    elif source == "panel":
        values = ins[0][...].astype(F32)
    else:
        values = jnp.where(idx[step, 1] == 1, joined(ins[1:]), ins[0][...].astype(F32))
    outs[0][...] = values.astype(BF)
    scale = lax.rsqrt(jnp.mean(values * values, axis=-1, keepdims=True) + 1e-05)
    normed = (values * scale * gain[...]).astype(BF)
    packed = dot(table[idx[step, 0]], normed)
    for d in range(EXPERTS):
        outs[1 + d][...] = packed[d * PAD : (d + 1) * PAD].astype(BF)


def combine_kernel(step, idx, panel, hi, lo, b0, b1, b2, b3, produced):
    here = idx[step, 0]
    rows = stacked((b0, b1, b2, b3))
    mixed = dot(hi[here], rows) + dot(lo[here], rows)
    produced[...] = (panel[...].astype(F32) + mixed).astype(BF)


def tighten_kernel(b0, b1, b2, b3, out):
    rows = stacked((b0, b1, b2, b3))
    i = lax.broadcasted_iota(jnp.int32, (EXPERTS * MOST, EXPERTS * PAD), 0)
    j = lax.broadcasted_iota(jnp.int32, (EXPERTS * MOST, EXPERTS * PAD), 1)
    pick = (j == i + (i // MOST) * (PAD - MOST)).astype(F32).astype(BF)
    out[...] = dot(pick, rows).astype(BF)


def spread_kernel(own, r1, r2, r3, *outs):
    total = own[...].astype(F32) + r1[...].astype(F32) + r2[...].astype(F32) + r3[...].astype(F32)
    i = lax.broadcasted_iota(jnp.int32, (EXPERTS * PAD, EXPERTS * MOST), 0)
    j = lax.broadcasted_iota(jnp.int32, (EXPERTS * PAD, EXPERTS * MOST), 1)
    inside = (i % PAD) < MOST
    pick = ((i == j + (j // MOST) * (PAD - MOST)) & inside).astype(F32).astype(BF)
    blocks = dot(pick, total.astype(BF))
    for d, out in enumerate(outs):
        out[...] = blocks[d * PAD : (d + 1) * PAD].astype(BF)


def pair_kernel(own, other, *outs):
    n = outs[0].shape[0]
    for d, out in enumerate(outs):
        total = own[...].astype(F32)[d * n : (d + 1) * n] + other[...].astype(F32)[d * n : (d + 1) * n]
        out[...] = total.astype(BF)


def experts_kernel(order, *refs):
    rows, (up, down, keep, give, narrow, hid, wide) = refs[:-7], refs[-7:]
    width, units = up.shape
    n = keep.shape[0] // 4
    cols = wide.shape[1]
    if len(rows) == 8:
        for i in range(width // cols):
            at = pl.ds(i * cols, cols)
            for b in range(8):
                wide[b * n : (b + 1) * n, :] = rows[b][:, at].astype(F32)
            narrow[:, at] = wide[...].astype(BF)
        source = narrow
    else:
        source = rows[0]
    part = 256
    for i in range(units // part):
        at = pl.ds(i * part, part)
        v = dot(source[...], up[:, at])
        hid[:, at] = (v / (1.0 + jnp.exp(-v))).astype(BF)
    for i in range(width // cols):
        at = pl.ds(i * cols, cols)
        out = dot(hid[...], down[:, at])
        if len(rows) == 8:
            keep[:, at] = out[: 4 * n].astype(BF)
            give[:, at] = out[4 * n :].astype(BF)
        else:
            wide[...] = out
            for to, row in ((keep, 0), (give, 1)):
                picked = [wide[pl.ds(pl.multiple_of(order[row, d] * n, n), n), :] for d in range(4)]
                to[:, at] = jnp.concatenate(picked, axis=0).astype(BF)


SMEM = pl.BlockSpec(memory_space=pltpu.SMEM)


class Line:
    def call(self, kernel, outs, args, name, first=0, micro=None, scratch=(), limit=8, after=(), **extra):
        specs = [SMEM] * first + whole(len(args) - first)
        if micro is not None:
            specs[-4:] = [pl.BlockSpec((1, *a.shape[1:]), lambda i: (micro, 0, 0)) for a in args[-4:]]
            extra["grid"] = (1,)
        n_in, n_skip = len(args), len(after)

        def body(*refs):
            kernel(*refs[:n_in], *refs[n_in + n_skip :])

        return pl.pallas_call(
            body,
            out_shape=[jax.ShapeDtypeStruct(s, BF) for s in outs],
            in_specs=specs + [pl.BlockSpec(memory_space=pl.ANY)] * n_skip,
            out_specs=whole(len(outs)),
            scratch_shapes=list(scratch),
            compiler_params=pltpu.CompilerParams(vmem_limit_bytes=limit * 2**20),
            name=name,
            **extra,
        )(*args, *after)

    def experts(self, order, rows, up, down):
        width, units = up.shape
        n = sum(r.shape[0] for r in rows)
        return self.call(
            experts_kernel,
            [(n // 2, width)] * 2,
            [order, *rows, up, down],
            "experts",
            1,
            scratch=[
                pltpu.VMEM((n, width) if len(rows) > 1 else (16, 128), BF),
                pltpu.VMEM((n, units), BF),
                pltpu.VMEM((n, 768), F32),
            ],
            limit=LIMIT,
            cost_estimate=pl.CostEstimate(
                flops=4 * n * width * units, bytes_accessed=4 * n * width, transcendentals=n * units
            ),
        )


def slots_of(chosen, y):
    micro, tok, top = chosen.shape
    flat = chosen.reshape(micro, tok * top)
    order = jnp.arange(tok * top)
    same = (flat[:, :, None] == flat[:, None, :]) & (order[None, :, None] > order[None, None, :])
    rank = jnp.sum(same.astype(jnp.int32), axis=2).reshape(chosen.shape)
    distance = (chosen - y + EXPERTS) % EXPERTS
    return jnp.where(chosen < EXPERTS, distance * PAD + rank, -1)


def on_device(inputs, gain, w_up, w_down, routes, route_weight):
    micro, tok, _ = inputs.shape
    width = gain.shape[1]
    z, y, x, core = (lax.axis_index(a) for a in ("pipe", "y", "x", "core"))
    slots = EXPERTS * MOST
    block, column, panel_shape = (PAD, width), (slots, width), (tok, width)

    def gathered(part):
        return [part] + [lax.ppermute(part, "pipe", [(i, 0)]) for i in range(1, SECTIONS)]

    early, late = gathered(inputs[:STREAMS]), gathered(inputs[STREAMS:])

    def fresh(m):
        return (m, early) if m < STREAMS else (m - STREAMS, late)

    gain_row = gain.astype(F32)
    ids = jnp.arange(EXPERTS * PAD, dtype=jnp.int32)
    slot = slots_of(routes[0], y)
    table = jnp.any(slot[:, None, :, :] == ids[None, :, None, None], axis=3).astype(BF)
    weight = jnp.sum(jnp.where(slot[:, :, :, None] == ids, route_weight[0][:, :, :, None], 0.0), axis=2)
    hi = weight.astype(BF)
    lo = (weight - hi.astype(F32)).astype(BF)
    order = jnp.stack(
        [jnp.stack([2 * ((x - d) % 4) + (core + c) % 2 for d in range(4)]) for c in range(2)]
    ).astype(jnp.int32)

    def indices(stream, count):
        rows = []
        for t in range(count + SECTIONS - 1):
            m = stream + STREAMS * jnp.clip(t - z, 0, count - 1)
            place = jnp.where((t - z >= 0) & (t - z < count), m, micro)
            rows.append(jnp.stack([m, (z == 0).astype(m.dtype), place]))
        return jnp.stack(rows).astype(jnp.int32)

    counts = [len(range(a, micro, STREAMS)) for a in range(STREAMS)]
    idx = [indices(a, counts[a]) for a in range(STREAMS)]
    line = Line()
    result = [jnp.zeros((micro + 1, tok, width), BF)]
    state = [{} for _ in range(STREAMS)]

    x_busy = []

    def on_x():
        return x_busy[-1] if x_busy else []

    def enter(a, t, s):
        given = [idx[a], gain_row, table]
        m = None
        source = "panel"
        if t:
            given.append(s["from_before"])
        if t < counts[a]:
            m, parts = fresh(a + STREAMS * t)
            given += parts
            source = "either" if t else "inputs"
        s["panel"], *blocks = line.call(
            functools.partial(enter_kernel, t, source), [panel_shape] + [block] * 4, given, "enter", 1, m
        )
        s["rows"] = [blocks[0]] + [moved(blocks[d], "y", d) for d in range(1, 4)]

    def tighten(a, t, s):
        (own,) = line.call(tighten_kernel, [column], s["rows"], "tighten")
        if GATHER:
            s["all"] = [lax.all_gather(own, ("x", "core"), tiled=True)]
        else:
            mine = [own] + [moved(own, "x", d) for d in range(1, 4)]
            x_busy.append(mine[1:])
            s["all"] = mine + [moved(v, "core", 1) for v in mine]

    def experts(a, t, s):
        s["keep"], give = line.experts(order, s["all"], w_up[0], w_down[0])
        s["back"] = moved(give, "core", 1)

    def pair(a, t, s):
        sums = line.call(pair_kernel, [column] * 4, [s["keep"], s["back"]], "pair")
        s["home"] = [sums[0]] + [moved(sums[d], "x", -d) for d in range(1, 4)]
        x_busy.append(s["home"][1:])

    def spread(a, t, s):
        blocks = line.call(spread_kernel, [block] * 4, s["home"], "spread")
        s["arrived"] = [blocks[0]] + [moved(blocks[d], "y", -d) for d in range(1, 4)]

    def combine(a, t, s):
        (made,) = line.call(
            functools.partial(combine_kernel, t), [panel_shape], [idx[a], s["panel"], hi, lo, *s["arrived"]], "combine", 1
        )
        if t < counts[a] + SECTIONS - 2:
            s["from_before"] = lax.ppermute(made, "pipe", [(i, i + 1) for i in range(SECTIONS - 1)])
        result[0] = lax.dynamic_update_index_in_dim(result[0], made, idx[a][t, 2], 0)

    stages = (enter, tighten, experts, pair, spread, combine)
    plan = []
    for a in range(STREAMS):
        for t in range(counts[a] + SECTIONS - 1):
            for at, stage in zip(PHASES, stages):
                plan.append((t * PERIOD + a * OFFSET + at, a, t, stage))
    for _, a, t, stage in sorted(plan, key=lambda p: p[0]):
        stage(a, t, state[a])
    return result[0][None, :micro]


def solution(mesh):
    devices = mesh.devices
    wide = Mesh(devices.reshape(devices.shape[0], 4, 4, 2), ("pipe", "y", "x", "core"))
    ed = ("y", "x", "core")
    in_specs = (
        P(None, ed, "pipe"),
        P("pipe", None),
        P("pipe", None, ed),
        P("pipe", ed, None),
        P("pipe", None, ed, None),
        P("pipe", None, ed, None),
    )
    return jax.shard_map(
        on_device, mesh=wide, in_specs=in_specs, out_specs=P("pipe", None, ed, None), check_vma=False
    )
```

```python
import functools

import jax
import jax.numpy as jnp
from jax import lax
from jax.experimental import pallas as pl
from jax.experimental.pallas import tpu as pltpu
from jax.sharding import Mesh, PartitionSpec as P

EXPERTS = 4
MOST = 6
PAD = 8
STREAMS = 2
COST = 1
SECTIONS = 4
BF = jnp.bfloat16
F32 = jnp.float32


def dot(a, b):
    return jnp.dot(a, b, preferred_element_type=F32)


def whole(n):
    return [pl.BlockSpec(memory_space=pltpu.VMEM)] * n


def moved(value, axis, by):
    n = lax.axis_size(axis)
    return lax.ppermute(value, axis, [(i, (i + by) % n) for i in range(n)])


def stacked(refs):
    return jnp.concatenate([r[...].astype(F32) for r in refs], axis=0).astype(BF)


def joined(parts):
    return jnp.concatenate([p[0].astype(F32) for p in parts], axis=1)


def enter_kernel(step, source, idx, gain, table, *refs):
    ins, outs = refs[: len(refs) - 1 - EXPERTS], refs[len(refs) - 1 - EXPERTS :]
    if source == "inputs":
        values = joined(ins)
    elif source == "panel":
        values = ins[0][...].astype(F32)
    else:
        values = jnp.where(idx[step, 1] == 1, joined(ins[1:]), ins[0][...].astype(F32))
    outs[0][...] = values.astype(BF)
    scale = lax.rsqrt(jnp.mean(values * values, axis=-1, keepdims=True) + 1e-05)
    normed = (values * scale * gain[...]).astype(BF)
    packed = dot(table[idx[step, 0]], normed)
    for d in range(EXPERTS):
        outs[1 + d][...] = packed[d * PAD : (d + 1) * PAD].astype(BF)


def combine_kernel(step, idx, panel, hi, lo, b0, b1, b2, b3, produced):
    here = idx[step, 0]
    rows = stacked((b0, b1, b2, b3))
    mixed = dot(hi[here], rows) + dot(lo[here], rows)
    produced[...] = (panel[...].astype(F32) + mixed).astype(BF)


def tighten_kernel(b0, b1, b2, b3, out):
    rows = stacked((b0, b1, b2, b3))
    i = lax.broadcasted_iota(jnp.int32, (EXPERTS * MOST, EXPERTS * PAD), 0)
    j = lax.broadcasted_iota(jnp.int32, (EXPERTS * MOST, EXPERTS * PAD), 1)
    pick = (j == i + (i // MOST) * (PAD - MOST)).astype(F32).astype(BF)
    out[...] = dot(pick, rows).astype(BF)


def spread_kernel(own, r1, r2, r3, *outs):
    total = own[...].astype(F32) + r1[...].astype(F32) + r2[...].astype(F32) + r3[...].astype(F32)
    i = lax.broadcasted_iota(jnp.int32, (EXPERTS * PAD, EXPERTS * MOST), 0)
    j = lax.broadcasted_iota(jnp.int32, (EXPERTS * PAD, EXPERTS * MOST), 1)
    inside = (i % PAD) < MOST
    pick = ((i == j + (j // MOST) * (PAD - MOST)) & inside).astype(F32).astype(BF)
    blocks = dot(pick, total.astype(BF))
    for d, out in enumerate(outs):
        out[...] = blocks[d * PAD : (d + 1) * PAD].astype(BF)


def pair_kernel(own, other, *outs):
    n = outs[0].shape[0]
    for d, out in enumerate(outs):
        total = own[...].astype(F32)[d * n : (d + 1) * n] + other[...].astype(F32)[d * n : (d + 1) * n]
        out[...] = total.astype(BF)


def stack_kernel(own, r1, r2, r3, out):
    out[...] = stacked((own, r1, r2, r3))


def experts_kernel(mine, theirs, up, down, keep, give, hid):
    width, units = up.shape
    half = mine.shape[0]
    rows = jnp.concatenate([mine[...], theirs[...]], axis=0)
    part = 256
    for i in range(units // part):
        at = pl.ds(i * part, part)
        v = dot(rows, up[:, at])
        hid[:, at] = (v / (1.0 + jnp.exp(-v))).astype(BF)
    part = 768
    for i in range(width // part):
        at = pl.ds(i * part, part)
        out = dot(hid[...], down[:, at])
        keep[:, at] = out[:half].astype(BF)
        give[:, at] = out[half:].astype(BF)


SMEM = pl.BlockSpec(memory_space=pltpu.SMEM)


class Line:
    def __init__(self):
        self.token = jnp.zeros((8, 128), F32)

    def call(self, kernel, outs, args, name, first=0, micro=None, scratch=(), limit=6, **extra):
        specs = [SMEM] * first + whole(len(args) - first)
        if micro is not None:
            specs[-4:] = [pl.BlockSpec((1, *a.shape[1:]), lambda i: (micro, 0, 0)) for a in args[-4:]]
            extra["grid"] = (1,)
        n_in, n_out = len(args), len(outs)

        def body(*refs):
            before, after = refs[n_in], refs[n_in + 1 + n_out]
            kernel(*refs[:n_in], *refs[n_in + 1 : n_in + 1 + n_out], *refs[n_in + 2 + n_out :])
            after[...] = before[...]

        *result, self.token = pl.pallas_call(
            body,
            out_shape=[jax.ShapeDtypeStruct(s, BF) for s in outs] + [jax.ShapeDtypeStruct((8, 128), F32)],
            in_specs=specs + whole(1),
            out_specs=whole(n_out + 1),
            scratch_shapes=list(scratch),
            compiler_params=pltpu.CompilerParams(vmem_limit_bytes=limit * 2**20),
            cost_estimate=pl.CostEstimate(flops=COST, bytes_accessed=COST, transcendentals=0),
            name=name,
            **extra,
        )(*args, self.token)
        return result

    def experts(self, rows, up, down):
        width, units = up.shape
        half = rows[0].shape[0]
        return self.call(
            experts_kernel,
            [(half, width)] * 2,
            [*rows, up, down],
            "experts",
            scratch=[pltpu.VMEM((2 * half, units), BF)],
            limit=10,
        )


def slots_of(chosen, y):
    micro, tok, top = chosen.shape
    flat = chosen.reshape(micro, tok * top)
    order = jnp.arange(tok * top)
    same = (flat[:, :, None] == flat[:, None, :]) & (order[None, :, None] > order[None, None, :])
    rank = jnp.sum(same.astype(jnp.int32), axis=2).reshape(chosen.shape)
    distance = (chosen - y + EXPERTS) % EXPERTS
    return jnp.where(chosen < EXPERTS, distance * PAD + rank, -1)


STAGES = (
    (1.0, 3.5, "y", 4.0, 3.5),
    (0.3, 4.0, "x", 11.8, 2.5),
    (0.5, 0.3, "core", 2.0, 0.8),
    (5.9, 0.3, "core", 2.0, 0.8),
    (0.4, 4.0, "x", 11.8, 2.5),
    (0.3, 3.5, "y", 4.0, 3.5),
    (0.9, 1.5, "pipe", 4.0, 4.0),
)


def planned(totals):
    done, ready, links = [0] * len(totals), [0.0] * len(totals), {}
    now, order = 0.0, []
    while len(order) < sum(totals):
        left = [a for a in range(len(totals)) if done[a] < totals[a]]
        a = min(left, key=lambda a: (max(now, ready[a]), done[a] - totals[a]))
        kernel, starts, link, busy, latency = STAGES[done[a] % len(STAGES)]
        now = max(now, ready[a]) + kernel
        links[link] = max(now + 0.4 * starts, links.get(link, 0.0)) + busy
        ready[a] = max(links[link] + latency, now + starts)
        now += starts
        done[a] += 1
        order.append(a)
    return order


def on_device(inputs, gain, w_up, w_down, routes, route_weight):
    micro, tok, _ = inputs.shape
    width = gain.shape[1]
    z, y = lax.axis_index("pipe"), lax.axis_index("y")
    slots = EXPERTS * MOST
    block, column, panel_shape = (PAD, width), (slots, width), (tok, width)

    def gathered(part):
        return [part] + [lax.ppermute(part, "pipe", [(i, 0)]) for i in range(1, SECTIONS)]

    early, late = gathered(inputs[:STREAMS]), gathered(inputs[STREAMS:])

    def fresh(m):
        return (m, early) if m < STREAMS else (m - STREAMS, late)

    gain_row = gain.astype(F32)
    ids = jnp.arange(EXPERTS * PAD, dtype=jnp.int32)
    slot = slots_of(routes[0], y)
    table = jnp.any(slot[:, None, :, :] == ids[None, :, None, None], axis=3).astype(BF)
    weight = jnp.sum(jnp.where(slot[:, :, :, None] == ids, route_weight[0][:, :, :, None], 0.0), axis=2)
    hi = weight.astype(BF)
    lo = (weight - hi.astype(F32)).astype(BF)
    def indices(stream, count):
        rows = []
        for t in range(count + SECTIONS - 1):
            m = stream + STREAMS * jnp.clip(t - z, 0, count - 1)
            rows.append(jnp.stack([m, (z == 0).astype(m.dtype)]))
        return jnp.stack(rows).astype(jnp.int32)

    def place(stream, t):
        m = t - z
        return jnp.where((m >= 0) & (m < counts[stream]), stream + STREAMS * m, micro)

    counts = [len(range(a, micro, STREAMS)) for a in range(STREAMS)]
    idx = [indices(a, counts[a]) for a in range(STREAMS)]
    line = Line()
    result = [jnp.zeros((micro + 1, tok, width), BF)]
    state = [{} for _ in range(STREAMS)]

    def enter(a, t, s):
        given = [idx[a], gain_row, table]
        m = None
        source = "panel"
        if t:
            given.append(s["from_before"])
        if t < counts[a]:
            m, parts = fresh(a + STREAMS * t)
            given += parts
            source = "either" if t else "inputs"
        s["panel"], *blocks = line.call(
            functools.partial(enter_kernel, t, source), [panel_shape] + [block] * 4, given, "enter", 1, m
        )
        s["rows"] = [blocks[0]] + [moved(blocks[d], "y", d) for d in range(1, 4)]

    def tighten(a, t, s):
        (own,) = line.call(tighten_kernel, [column], s["rows"], "tighten")
        s["along_x"] = [own] + [moved(own, "x", d) for d in range(1, 4)]

    def stack(a, t, s):
        (s["mine"],) = line.call(stack_kernel, [(4 * slots, width)], s["along_x"], "stack")
        s["theirs"] = moved(s["mine"], "core", 1)

    def experts(a, t, s):
        s["keep"], give = line.experts((s["mine"], s["theirs"]), w_up[0], w_down[0])
        s["back"] = moved(give, "core", 1)

    def pair(a, t, s):
        sums = line.call(pair_kernel, [column] * 4, [s["keep"], s["back"]], "pair")
        s["home"] = [sums[0]] + [moved(sums[d], "x", -d) for d in range(1, 4)]

    def spread(a, t, s):
        blocks = line.call(spread_kernel, [block] * 4, s["home"], "spread")
        s["arrived"] = [blocks[0]] + [moved(blocks[d], "y", -d) for d in range(1, 4)]

    def combine(a, t, s):
        (made,) = line.call(
            functools.partial(combine_kernel, t), [panel_shape], [idx[a], s["panel"], hi, lo, *s["arrived"]], "combine", 1
        )
        if t < counts[a] + SECTIONS - 2:
            s["from_before"] = lax.ppermute(made, "pipe", [(i, i + 1) for i in range(SECTIONS - 1)])
        result[0] = lax.dynamic_update_index_in_dim(result[0], made, place(a, t), 0)

    stages = (enter, tighten, stack, experts, pair, spread, combine)
    done = [0] * STREAMS
    n = (counts[0] + SECTIONS - 1) * len(stages)
    lead = 1
    for a in [0] * lead + [0, 1] * (n - lead) + [1] * lead:
        t, i = divmod(done[a], len(stages))
        done[a] += 1
        stages[i](a, t, state[a])
    return result[0][None, :micro]


def solution(mesh):
    devices = mesh.devices
    wide = Mesh(devices.reshape(devices.shape[0], 4, 4, 2), ("pipe", "y", "x", "core"))
    ed = ("y", "x", "core")
    in_specs = (
        P(None, ed, "pipe"),
        P("pipe", None),
        P("pipe", None, ed),
        P("pipe", ed, None),
        P("pipe", None, ed, None),
        P("pipe", None, ed, None),
    )
    return jax.shard_map(
        on_device, mesh=wide, in_specs=in_specs, out_specs=P("pipe", None, ed, None), check_vma=False
    )
```

```python
import functools

import jax
import jax.numpy as jnp
from jax import lax
from jax.experimental import pallas as pl
from jax.experimental.pallas import tpu as pltpu
from jax.sharding import Mesh, PartitionSpec as P

EXPERTS = 4
MOST = 6
PAD = 8
STREAMS = 2
COST = 1
LEAD = 1
PATTERN = (0, 1, 0, 0, 1, 0, 0, 1, 1, 0, 1, 1, 0, 1, 0, 1)
SECTIONS = 4
BF = jnp.bfloat16
F32 = jnp.float32


def dot(a, b):
    return jnp.dot(a, b, preferred_element_type=F32)


def whole(n):
    return [pl.BlockSpec(memory_space=pltpu.VMEM)] * n


def moved(value, axis, by):
    n = lax.axis_size(axis)
    return lax.ppermute(value, axis, [(i, (i + by) % n) for i in range(n)])


def stacked(refs):
    return jnp.concatenate([r[...].astype(F32) for r in refs], axis=0).astype(BF)


def joined(parts):
    return jnp.concatenate([p[0].astype(F32) for p in parts], axis=1)


def enter_kernel(step, source, idx, gain, table, *refs):
    ins, outs = refs[: len(refs) - 1 - EXPERTS], refs[len(refs) - 1 - EXPERTS :]
    if source == "inputs":
        values = joined(ins)
    elif source == "panel":
        values = ins[0][...].astype(F32)
    else:
        values = jnp.where(idx[step, 1] == 1, joined(ins[1:]), ins[0][...].astype(F32))
    outs[0][...] = values.astype(BF)
    scale = lax.rsqrt(jnp.mean(values * values, axis=-1, keepdims=True) + 1e-05)
    normed = (values * scale * gain[...]).astype(BF)
    packed = dot(table[idx[step, 0]], normed)
    for d in range(EXPERTS):
        outs[1 + d][...] = packed[d * PAD : (d + 1) * PAD].astype(BF)


def combine_kernel(step, idx, panel, hi, lo, b0, b1, b2, b3, produced):
    here = idx[step, 0]
    rows = stacked((b0, b1, b2, b3))
    mixed = dot(hi[here], rows) + dot(lo[here], rows)
    produced[...] = (panel[...].astype(F32) + mixed).astype(BF)


def tighten_kernel(b0, b1, b2, b3, out):
    rows = stacked((b0, b1, b2, b3))
    i = lax.broadcasted_iota(jnp.int32, (EXPERTS * MOST, EXPERTS * PAD), 0)
    j = lax.broadcasted_iota(jnp.int32, (EXPERTS * MOST, EXPERTS * PAD), 1)
    pick = (j == i + (i // MOST) * (PAD - MOST)).astype(F32).astype(BF)
    out[...] = dot(pick, rows).astype(BF)


def spread_kernel(own, r1, r2, r3, *outs):
    total = own[...].astype(F32) + r1[...].astype(F32) + r2[...].astype(F32) + r3[...].astype(F32)
    i = lax.broadcasted_iota(jnp.int32, (EXPERTS * PAD, EXPERTS * MOST), 0)
    j = lax.broadcasted_iota(jnp.int32, (EXPERTS * PAD, EXPERTS * MOST), 1)
    inside = (i % PAD) < MOST
    pick = ((i == j + (j // MOST) * (PAD - MOST)) & inside).astype(F32).astype(BF)
    blocks = dot(pick, total.astype(BF))
    for d, out in enumerate(outs):
        out[...] = blocks[d * PAD : (d + 1) * PAD].astype(BF)


def pair_kernel(own, other, *outs):
    n = outs[0].shape[0]
    for d, out in enumerate(outs):
        total = own[...].astype(F32)[d * n : (d + 1) * n] + other[...].astype(F32)[d * n : (d + 1) * n]
        out[...] = total.astype(BF)


def copy_kernel(given, made):
    made[...] = given[...]


def stack_kernel(own, r1, r2, r3, out):
    out[...] = stacked((own, r1, r2, r3))


def experts_kernel(mine, theirs, up, down, keep, give, hid):
    width, units = up.shape
    half = mine.shape[0]
    rows = jnp.concatenate([mine[...], theirs[...]], axis=0)
    part = 256
    for i in range(units // part):
        at = pl.ds(i * part, part)
        v = dot(rows, up[:, at])
        hid[:, at] = (v / (1.0 + jnp.exp(-v))).astype(BF)
    part = 768
    for i in range(width // part):
        at = pl.ds(i * part, part)
        out = dot(hid[...], down[:, at])
        keep[:, at] = out[:half].astype(BF)
        give[:, at] = out[half:].astype(BF)


SMEM = pl.BlockSpec(memory_space=pltpu.SMEM)


class Line:
    def __init__(self):
        self.token = jnp.zeros((8, 128), F32)

    def call(self, kernel, outs, args, name, first=0, micro=None, scratch=(), limit=6, **extra):
        specs = [SMEM] * first + whole(len(args) - first)
        if micro is not None:
            specs[-4:] = [pl.BlockSpec((1, *a.shape[1:]), lambda i: (micro, 0, 0)) for a in args[-4:]]
            extra["grid"] = (1,)
        n_in, n_out = len(args), len(outs)

        def body(*refs):
            before, after = refs[n_in], refs[n_in + 1 + n_out]
            kernel(*refs[:n_in], *refs[n_in + 1 : n_in + 1 + n_out], *refs[n_in + 2 + n_out :])
            after[...] = before[...]

        *result, self.token = pl.pallas_call(
            body,
            out_shape=[jax.ShapeDtypeStruct(s, BF) for s in outs] + [jax.ShapeDtypeStruct((8, 128), F32)],
            in_specs=specs + whole(1),
            out_specs=whole(n_out + 1),
            scratch_shapes=list(scratch),
            compiler_params=pltpu.CompilerParams(vmem_limit_bytes=limit * 2**20),
            cost_estimate=pl.CostEstimate(flops=COST, bytes_accessed=COST, transcendentals=0),
            name=name,
            **extra,
        )(*args, self.token)
        return result

    def mark(self, value):
        return self.call(copy_kernel, [value.shape], [value], "mark")[0]

    def experts(self, rows, up, down):
        width, units = up.shape
        half = rows[0].shape[0]
        return self.call(
            experts_kernel,
            [(half, width)] * 2,
            [*rows, up, down],
            "experts",
            scratch=[pltpu.VMEM((2 * half, units), BF)],
            limit=10,
        )


def slots_of(chosen, y):
    micro, tok, top = chosen.shape
    flat = chosen.reshape(micro, tok * top)
    order = jnp.arange(tok * top)
    same = (flat[:, :, None] == flat[:, None, :]) & (order[None, :, None] > order[None, None, :])
    rank = jnp.sum(same.astype(jnp.int32), axis=2).reshape(chosen.shape)
    distance = (chosen - y + EXPERTS) % EXPERTS
    return jnp.where(chosen < EXPERTS, distance * PAD + rank, -1)


def planned(totals):
    order, left = [0] * LEAD, [totals[0] - LEAD, totals[1]]
    while any(left):
        for a in PATTERN:
            if left[a]:
                order.append(a)
                left[a] -= 1
    return order


def on_device(inputs, gain, w_up, w_down, routes, route_weight):
    micro, tok, _ = inputs.shape
    width = gain.shape[1]
    z, y = lax.axis_index("pipe"), lax.axis_index("y")
    slots = EXPERTS * MOST
    block, column, panel_shape = (PAD, width), (slots, width), (tok, width)

    def gathered(part):
        return [part] + [lax.ppermute(part, "pipe", [(i, 0)]) for i in range(1, SECTIONS)]

    early, late = gathered(inputs[:STREAMS]), gathered(inputs[STREAMS:])

    def fresh(m):
        return (m, early) if m < STREAMS else (m - STREAMS, late)

    gain_row = gain.astype(F32)
    ids = jnp.arange(EXPERTS * PAD, dtype=jnp.int32)
    slot = slots_of(routes[0], y)
    table = jnp.any(slot[:, None, :, :] == ids[None, :, None, None], axis=3).astype(BF)
    weight = jnp.sum(jnp.where(slot[:, :, :, None] == ids, route_weight[0][:, :, :, None], 0.0), axis=2)
    hi = weight.astype(BF)
    lo = (weight - hi.astype(F32)).astype(BF)
    def indices(stream, count):
        rows = []
        for t in range(count + SECTIONS - 1):
            m = stream + STREAMS * jnp.clip(t - z, 0, count - 1)
            rows.append(jnp.stack([m, (z == 0).astype(m.dtype)]))
        return jnp.stack(rows).astype(jnp.int32)

    def place(stream, t):
        m = t - z
        return jnp.where((m >= 0) & (m < counts[stream]), stream + STREAMS * m, micro)

    counts = [len(range(a, micro, STREAMS)) for a in range(STREAMS)]
    idx = [indices(a, counts[a]) for a in range(STREAMS)]
    line = Line()
    result = [jnp.zeros((micro + 1, tok, width), BF)]
    state = [{} for _ in range(STREAMS)]

    def enter(a, t, s):
        given = [idx[a], gain_row, table]
        m = None
        source = "panel"
        if t:
            given.append(s["from_before"])
        if t < counts[a]:
            m, parts = fresh(a + STREAMS * t)
            given += parts
            source = "either" if t else "inputs"
        s["panel"], *blocks = line.call(
            functools.partial(enter_kernel, t, source), [panel_shape] + [block] * 4, given, "enter", 1, m
        )
        s["rows"] = [blocks[0]] + [moved(blocks[d], "y", d) for d in range(1, 4)]

    def tighten(a, t, s):
        (own,) = line.call(tighten_kernel, [column], s["rows"], "tighten")
        s["along_x"] = [own] + [moved(own, "x", d) for d in range(1, 4)]

    def stack(a, t, s):
        (s["mine"],) = line.call(stack_kernel, [(4 * slots, width)], s["along_x"], "stack")
        s["theirs"] = moved(s["mine"], "core", 1)

    def experts(a, t, s):
        s["keep"], s["give"] = line.experts((s["mine"], s["theirs"]), w_up[0], w_down[0])

    def swap(a, t, s):
        s["back"] = moved(line.mark(s["give"]), "core", 1)

    def pair(a, t, s):
        sums = line.call(pair_kernel, [column] * 4, [s["keep"], s["back"]], "pair")
        s["home"] = [sums[0]] + [moved(sums[d], "x", -d) for d in range(1, 4)]

    def spread(a, t, s):
        blocks = line.call(spread_kernel, [block] * 4, s["home"], "spread")
        s["arrived"] = [blocks[0]] + [moved(blocks[d], "y", -d) for d in range(1, 4)]

    def combine(a, t, s):
        (made,) = line.call(
            functools.partial(combine_kernel, t), [panel_shape], [idx[a], s["panel"], hi, lo, *s["arrived"]], "combine", 1
        )
        if t < counts[a] + SECTIONS - 2:
            s["from_before"] = lax.ppermute(made, "pipe", [(i, i + 1) for i in range(SECTIONS - 1)])
        result[0] = lax.dynamic_update_index_in_dim(result[0], made, place(a, t), 0)

    stages = (enter, tighten, stack, experts, swap, pair, spread, combine)
    done = [0] * STREAMS
    for a in planned([(c + SECTIONS - 1) * len(stages) for c in counts]):
        t, i = divmod(done[a], len(stages))
        done[a] += 1
        stages[i](a, t, state[a])
    return result[0][None, :micro]


def solution(mesh):
    devices = mesh.devices
    wide = Mesh(devices.reshape(devices.shape[0], 4, 4, 2), ("pipe", "y", "x", "core"))
    ed = ("y", "x", "core")
    in_specs = (
        P(None, ed, "pipe"),
        P("pipe", None),
        P("pipe", None, ed),
        P("pipe", ed, None),
        P("pipe", None, ed, None),
        P("pipe", None, ed, None),
    )
    return jax.shard_map(
        on_device, mesh=wide, in_specs=in_specs, out_specs=P("pipe", None, ed, None), check_vma=False
    )
```
